32 devices in a mesh: dp: 4 (over z), seq: 2 (over y), head: 4 (over x, core).
Axes of the slice: x: 2, y: 2, z: 4, core: 2. Of those that a mesh axis runs over, the one named last changes fastest.
Arguments:
- frames: bfloat16 [4, 1536, 768], P('dp', 'seq'), may hold values from -6 to 6
- lengths: int32 [4], P('dp'), may hold values from 1152 to 1536, as said below
- grad_out: bfloat16 [4, 1536, 768], P('dp', 'seq'), may hold values from -6 to 6
- w_qkv: bfloat16 [2, 3, 768, 768], P(None, None, 'seq', 'head'), may hold values from -0.21875 to 0.21875
- qv_bias: bfloat16 [2, 2, 768], P(None, None, 'head'), may hold values from -0.75 to 0.75
- w_out: bfloat16 [2, 768, 768], P(None, 'head', 'seq'), may hold values from -6 to 6
- w_up: bfloat16 [2, 768, 3072], P(None, 'seq', 'head'), may hold values from -0.21875 to 0.21875
- up_bias: bfloat16 [2, 3072], P(None, 'head'), may hold values from -4 to 4
- w_down: bfloat16 [2, 3072, 768], P(None, 'head', 'seq'), may hold values from -0.109375 to 0.109375
- gains: bfloat16 [2, 2, 768], P(None, None, 'seq'), may hold values from 0.25 to 1.75
- shifts: bfloat16 [2, 4, 768], P(None, None, 'seq'), may hold values from -4 to 4
Outputs:
- out: bfloat16 [4, 1536, 768], P('dp', 'seq')
- grad_frames: float32 [4, 1536, 768], P('dp', 'seq')
- grad_w_qkv: float32 [2, 3, 768, 768], P(None, None, 'seq', 'head')
- grad_qv_bias: float32 [2, 2, 768], P(None, None, 'head')
- grad_w_out: float32 [2, 768, 768], P(None, 'head', 'seq')
- grad_w_up: float32 [2, 768, 3072], P(None, 'seq', 'head')
- grad_up_bias: float32 [2, 3072], P(None, 'head')
- grad_w_down: float32 [2, 3072, 768], P(None, 'head', 'seq')
- grad_gains: float32 [2, 2, 768], P(None, None, 'seq')
- grad_shifts: float32 [2, 4, 768], P(None, None, 'seq')
The draws below stay inside these ranges and needn't reach their ends.
Inputs may be any that keep to these rules, and one draw needn't show every extreme that they name: `lengths`: each clip's number of valid frames; keys at or past it are masked; some clip has all 1536 frames valid.
All inputs are finite; a program needn't handle non-finite values.
Results may differ from the reference program's by a relative error of at most 0.018.
Values may be sent and summed in bfloat16 or wider, within the bound.
A program may use at most 192 MiB of HBM per device.

```python
import jax
import jax.numpy as jnp
from jax import lax

D = 768
HEADS = 12
HD = 64
FF = 3072
FRAMES = 1536
LAYERS = 2
CLIPS = 4
FR_DEV = 768


def draw_lengths(key, part):
    key = jax.random.fold_in(key, 7)
    key_list = jax.random.split(key, 3)
    lowest = FRAMES - FR_DEV // 2
    drawn = jax.random.randint(key_list[0], (CLIPS,), lowest, FRAMES + 1)
    first_clip = jax.random.randint(key_list[1], (), 0, CLIPS)
    second_clip = (first_clip + jax.random.randint(key_list[2], (), 1, CLIPS)) % CLIPS
    slots = jnp.arange(CLIPS)
    drawn = jnp.where(slots == first_clip, FRAMES, drawn)
    drawn = jnp.where(slots == second_clip, lowest, drawn)
    return drawn.astype(jnp.int32)


def steps_of(stream_key, extent, shards, smallest, largest):
    gain, own = 1.0, jax.random.fold_in(stream_key, 6)
    for position, parts in shards:
        steps = jnp.exp(jax.random.uniform(jax.random.fold_in(own, position), (parts,), jnp.float32, smallest / len(shards), largest / len(shards)))
        gain = gain * jnp.repeat(steps, extent[position] // parts).reshape([-1 if axis == position else 1 for axis in range(len(extent))])
    return gain


def centred(key, shape, spread, limit, cuts=(), kind=jnp.bfloat16):
    array = jax.random.normal(key, shape, jnp.float32) * spread
    if len(cuts) > 0:
        array = steps_of(key, shape, cuts, -0.22, 0.18) * array
    return jnp.clip(array, min=-limit, max=limit).astype(kind)


def setup_inputs(seed: int = 0) -> dict:
    streams_of = jax.random.split(jax.random.key(seed), 12)
    frames = centred(streams_of[0], (CLIPS, FRAMES, D), 1.0, 6.0, ((0, 4), (1, 2)))
    lengths = draw_lengths(jax.random.fold_in(streams_of[11], 71), 0)
    grad_out = centred(streams_of[2], (CLIPS, FRAMES, D), 1.0, 6.0, ((0, 4), (1, 2)))
    w_qkv = centred(streams_of[3], (LAYERS, 3, D, D), D ** -0.5, 0.21875, ((2, 2), (3, 4)))
    qv_bias = centred(streams_of[4], (LAYERS, 2, D), 0.05, 0.75, ((2, 4),))
    w_out = centred(streams_of[5], (LAYERS, D, D), (max(1, 3 * D // FRAMES)) ** -0.5, 6.0, ((1, 4), (2, 2)))
    w_up = centred(streams_of[6], (LAYERS, D, FF), D ** -0.5, 0.21875, ((1, 2), (2, 4)))
    up_bias = centred(streams_of[7], (LAYERS, FF), 0.3, 4.0, ((1, 4),))
    w_down = centred(streams_of[8], (LAYERS, FF, D), FF ** -0.5, 0.109375, ((1, 4), (2, 2)))
    gains = jnp.clip(1.0 + 0.15 * jax.random.normal(streams_of[9], (LAYERS, 2, D), jnp.float32), 0.25, 1.75).astype(jnp.bfloat16)
    shifts = centred(streams_of[10], (LAYERS, 4, D), 0.3, 4.0, ((2, 2),))
    return dict(frames=frames, lengths=lengths, grad_out=grad_out, w_qkv=w_qkv, qv_bias=qv_bias, w_out=w_out, w_up=w_up, up_bias=up_bias, w_down=w_down, gains=gains, shifts=shifts)


epsilon = 1e-05
highest = lax.Precision.HIGHEST

@jax.custom_vjp
def low(v):
    return lax.optimization_barrier(v.astype(jnp.bfloat16)).astype(jnp.float32)

@jax.custom_vjp
def low_back(v):
    return v

def low_keep(v):
    return (low(v), None)

def low_pass(kept, grad):
    return (grad,)

def back_keep(v):
    return (v, None)

def back_low(kept, grad):
    return (low(grad),)
low.defvjp(low_keep, low_pass)
low_back.defvjp(back_keep, back_low)

def normalize(values, gain_vector, shift_vector):
    row_mean = lax.optimization_barrier(jnp.mean(values, axis=-1, keepdims=True))
    centered = values - row_mean
    variance = lax.optimization_barrier(jnp.mean(centered * centered, axis=-1, keepdims=True))
    return centered * lax.rsqrt(variance + epsilon) * gain_vector + shift_vector

def product(left_side, right_side):
    return jnp.matmul(left_side, right_side, precision=highest)

def block(stream, key_valid, weight_set, layer_index):
    w_qkv, qv_bias, w_out, w_up, up_bias, w_down, gains, shifts = weight_set
    frame_count = stream.shape[0]
    normed = low(normalize(stream, gains[layer_index, 0], shifts[layer_index, 0]))
    projected = jnp.einsum('fd,kdc->kfc', normed, w_qkv[layer_index], precision=highest)
    queries = low(low_back((projected[0] + qv_bias[layer_index, 0]) * HD ** (-0.5)))
    key_rows = low(low_back(projected[1]))
    value_rows = low(low_back(projected[2] + qv_bias[layer_index, 1]))
    query_heads = queries.reshape(frame_count, HEADS, HD)
    key_heads = key_rows.reshape(frame_count, HEADS, HD)
    value_heads = value_rows.reshape(frame_count, HEADS, HD)
    scores = low_back(jnp.einsum('qhe,khe->hqk', query_heads, key_heads, precision=highest))
    scores = jnp.where(key_valid[None, None, :], scores, -1e+30)
    probabilities = low(jax.nn.softmax(scores, axis=-1))
    attended = jnp.einsum('hqk,khe->qhe', probabilities, value_heads, precision=highest)
    attended = low(low_back(attended.reshape(frame_count, D)))
    stream = stream + low_back(product(attended, w_out[layer_index]) + shifts[layer_index, 1])
    normed_two = low(normalize(stream, gains[layer_index, 1], shifts[layer_index, 2]))
    hidden_pre = low_back(product(normed_two, w_up[layer_index]) + up_bias[layer_index])
    activated = low(jax.nn.gelu(hidden_pre, approximate=False))
    return stream + low_back(product(activated, w_down[layer_index]) + shifts[layer_index, 3])

def reference(frames, lengths, grad_out, w_qkv, qv_bias, w_out, w_up, up_bias, w_down, gains, shifts):
    positions = jnp.arange(FRAMES, dtype=jnp.int32)
    key_valid = positions[None, :] < lengths.astype(jnp.int32)[:, None]

    def forward(stream, qkv_weight, bias_pair, out_weight, up_weight, bias_up, down_weight, gain_set, shift_set):
        weight_set = (qkv_weight, bias_pair, out_weight, up_weight, bias_up, down_weight, gain_set, shift_set)

        def one_clip(carried):
            clip_stream, clip_valid = carried
            for layer_index in range(LAYERS):
                clip_stream = block(clip_stream, clip_valid, weight_set, layer_index)
            return clip_stream
        return lax.map(jax.checkpoint(one_clip), (stream, key_valid))
    output, pullback = jax.vjp(forward, frames.astype(jnp.float32), w_qkv.astype(jnp.float32), qv_bias.astype(jnp.float32), w_out.astype(jnp.float32), w_up.astype(jnp.float32), up_bias.astype(jnp.float32), w_down.astype(jnp.float32), gains.astype(jnp.float32), shifts.astype(jnp.float32))
    gradients = pullback(grad_out.astype(jnp.float32))
    return (output.astype(jnp.bfloat16), gradients[0], gradients[1], gradients[2], gradients[3], gradients[4], gradients[5], gradients[6], gradients[7], gradients[8])
```

```python
import functools

import jax
import jax.numpy as jnp
from jax import lax
from jax.experimental import pallas as pl
from jax.experimental.pallas import tpu as pltpu
from jax.sharding import PartitionSpec as P

HD = 64


epsilon = 1e-05


def normalize(values, gain_vector, shift_vector):
    row_mean = jnp.mean(values, axis=-1, keepdims=True)
    centered = values - row_mean
    variance = jnp.mean(centered * centered, axis=-1, keepdims=True)
    return centered * lax.rsqrt(variance + epsilon) * gain_vector + shift_vector


def gelu_exact(values):
    return jax.nn.gelu(values, approximate=False)


def column_sum(values):
    return jnp.sum(values.astype(jnp.float32), axis=0)


def stack_member(collected, position):
    return jnp.stack([entry[position] for entry in collected])


NT = (((1,), (1,)), ((), ()))
NN = (((1,), (0,)), ((), ()))
VMEM = pl.BlockSpec(memory_space=pltpu.VMEM)
BIG = 48 * 1024 * 1024


def head_masks(shape, heads):
    column = lax.broadcasted_iota(jnp.int32, shape, 1)
    return [(column >= h * HD) & (column < (h + 1) * HD) for h in range(heads)]


def attend_kernel(heads, q_ref, k_ref, v_ref, bias_ref, out_ref, lse_ref, vt_ref):
    @pl.when(pl.program_id(0) == 0)
    def _():
        vt_ref[...] = v_ref[...].astype(jnp.float32).T.astype(jnp.bfloat16)

    queries = q_ref[...]
    zero = jnp.zeros_like(queries)
    parts = []
    for h, mask in enumerate(head_masks(queries.shape, heads)):
        scores = lax.dot_general(
            k_ref[...], jnp.where(mask, queries, zero), NT, preferred_element_type=jnp.float32
        )
        scores = scores + bias_ref[...]
        peak = jnp.max(scores, axis=0, keepdims=True)
        powered = jnp.exp(scores - peak)
        total = jnp.sum(powered, axis=0, keepdims=True)
        probs = (powered * (1.0 / total)).astype(jnp.bfloat16)
        parts.append(
            lax.dot_general(
                vt_ref[h * HD : (h + 1) * HD, :], probs, NN, preferred_element_type=jnp.float32
            )
        )
        lse_ref[0, h : h + 1, :] = peak + jnp.log(total)
    out_ref[...] = jnp.concatenate(parts, axis=0).T.astype(jnp.bfloat16)


def row_block(rows):
    return 256 if rows % 256 == 0 else rows


def attend(queries, key_all, value_all, bias):
    rows, width = queries.shape
    keys = key_all.shape[0]
    heads = width // HD
    block = row_block(rows)
    return pl.pallas_call(
        functools.partial(attend_kernel, heads),
        grid=(rows // block,),
        in_specs=[
            pl.BlockSpec((block, width), lambda i: (i, 0)),
            pl.BlockSpec((keys, width), lambda i: (0, 0)),
            pl.BlockSpec((keys, width), lambda i: (0, 0)),
            pl.BlockSpec((keys, 1), lambda i: (0, 0)),
        ],
        out_specs=[
            pl.BlockSpec((block, width), lambda i: (i, 0)),
            pl.BlockSpec((1, heads, block), lambda i: (i, 0, 0)),
        ],
        out_shape=[
            jax.ShapeDtypeStruct((rows, width), jnp.bfloat16),
            jax.ShapeDtypeStruct((rows // block, heads, block), jnp.float32),
        ],
        scratch_shapes=[pltpu.VMEM((width, keys), jnp.bfloat16)],
        compiler_params=pltpu.CompilerParams(vmem_limit_bytes=BIG),
        cost_estimate=pl.CostEstimate(
            flops=8 * rows * keys * width, bytes_accessed=6 * keys * width, transcendentals=rows * keys * heads
        ),
    )(queries, key_all, value_all, bias)


def attend_back_kernel(
    heads, q_ref, k_ref, v_ref, bias_ref, lse_ref, o_ref, do_ref,
    dq_ref, dk_ref, dv_ref, kt_ref, dk_sum, dv_sum,
):
    step = pl.program_id(0)

    @pl.when(step == 0)
    def _():
        kt_ref[...] = k_ref[...].astype(jnp.float32).T.astype(jnp.bfloat16)
        dk_sum[...] = jnp.zeros_like(dk_sum)
        dv_sum[...] = jnp.zeros_like(dv_sum)

    queries = q_ref[...]
    grads = do_ref[...]
    zero = jnp.zeros_like(queries)
    inner = (o_ref[...].astype(jnp.float32) * grads.astype(jnp.float32)).T
    parts = []
    for h, mask in enumerate(head_masks(queries.shape, heads)):
        q_head = jnp.where(mask, queries, zero)
        do_head = jnp.where(mask, grads, zero)
        delta = jnp.sum(inner[h * HD : (h + 1) * HD, :], axis=0, keepdims=True)
        scores = lax.dot_general(k_ref[...], q_head, NT, preferred_element_type=jnp.float32)
        probs = jnp.exp(scores + bias_ref[...] - lse_ref[0, h : h + 1, :])
        d_probs = lax.dot_general(v_ref[...], do_head, NT, preferred_element_type=jnp.float32)
        dv_sum[...] += jnp.dot(
            probs.astype(jnp.bfloat16), do_head, preferred_element_type=jnp.float32
        )
        d_scores = (probs * (d_probs - delta)).astype(jnp.bfloat16)
        dk_sum[...] += jnp.dot(d_scores, q_head, preferred_element_type=jnp.float32)
        parts.append(
            jnp.dot(
                kt_ref[h * HD : (h + 1) * HD, :], d_scores, preferred_element_type=jnp.float32
            )
        )
    d_query = jnp.concatenate(parts, axis=0).T.astype(jnp.bfloat16)
    dq_ref[...] = (d_query.astype(jnp.float32) * (HD ** (-0.5))).astype(jnp.bfloat16)

    @pl.when(step == pl.num_programs(0) - 1)
    def _():
        dk_ref[...] = dk_sum[...].astype(jnp.bfloat16)
        dv_ref[...] = dv_sum[...].astype(jnp.bfloat16)


def attend_back(queries, key_all, value_all, bias, logsum, attended, d_attended):
    rows, width = queries.shape
    keys = key_all.shape[0]
    heads = width // HD
    block = row_block(rows)
    row_spec = pl.BlockSpec((block, width), lambda i: (i, 0))
    key_spec = pl.BlockSpec((keys, width), lambda i: (0, 0))
    return pl.pallas_call(
        functools.partial(attend_back_kernel, heads),
        grid=(rows // block,),
        in_specs=[
            row_spec,
            key_spec,
            key_spec,
            pl.BlockSpec((keys, 1), lambda i: (0, 0)),
            pl.BlockSpec((1, heads, block), lambda i: (i, 0, 0)),
            row_spec,
            row_spec,
        ],
        out_specs=[row_spec, key_spec, key_spec],
        out_shape=[
            jax.ShapeDtypeStruct((rows, width), jnp.bfloat16),
            jax.ShapeDtypeStruct((keys, width), jnp.bfloat16),
            jax.ShapeDtypeStruct((keys, width), jnp.bfloat16),
        ],
        scratch_shapes=[
            pltpu.VMEM((width, keys), jnp.bfloat16),
            pltpu.VMEM((keys, width), jnp.float32),
            pltpu.VMEM((keys, width), jnp.float32),
        ],
        compiler_params=pltpu.CompilerParams(vmem_limit_bytes=BIG),
        cost_estimate=pl.CostEstimate(
            flops=20 * rows * keys * width, bytes_accessed=12 * keys * width, transcendentals=rows * keys * heads
        ),
    )(queries, key_all, value_all, bias, logsum, attended, d_attended)


def head_sum_kernel(dims, chunks, a_ref, w_ref, out_ref, first, landed, own, chip, crossed, last, done, send, recv):
    me = lax.axis_index("head")
    core = me % 2
    sibling = me + 1 - 2 * core
    across = (me + 2) % 4
    half = a_ref.shape[0] // 2
    size = half // chunks
    mine = core * half
    theirs = (1 - core) * half

    barrier = pltpu.get_barrier_semaphore()
    for other in (sibling, across):
        pl.semaphore_signal(
            barrier, inc=1, device_id={"head": other}, device_id_type=pl.DeviceIdType.MESH
        )

    def product(base):
        rows = pl.ds(pl.multiple_of(base, 16), size)
        return lax.dot_general(a_ref[rows, :], w_ref[...], dims, preferred_element_type=jnp.float32)

    def remote(source, target, stage, c, other):
        return pltpu.make_async_remote_copy(
            src_ref=source.at[c],
            dst_ref=target.at[c],
            send_sem=send.at[stage, c],
            recv_sem=recv.at[stage, c],
            device_id={"head": other},
            device_id_type=pl.DeviceIdType.MESH,
        )

    outward = [remote(first, landed, 0, c, sibling) for c in range(chunks)]
    cross = [remote(chip, crossed, 1, c, across) for c in range(chunks)]
    back = [remote(last, done, 2, c, sibling) for c in range(chunks)]
    for c in range(chunks):
        first[c] = product(theirs + c * size).astype(jnp.bfloat16)
        if c == 0:
            pl.semaphore_wait(barrier, 2)
        outward[c].start()
    for c in range(chunks):
        own[c] = product(mine + c * size)
        outward[c].wait_recv()
        chip[c] = (own[c] + landed[c].astype(jnp.float32)).astype(jnp.bfloat16)
        cross[c].start()
    for c in range(chunks):
        cross[c].wait_recv()
        total = (chip[c].astype(jnp.float32) + crossed[c].astype(jnp.float32)).astype(jnp.bfloat16)
        last[c] = total
        back[c].start()
        out_ref[pl.ds(pl.multiple_of(mine + c * size, 16), size), :] = total
    for c in range(chunks):
        back[c].wait_recv()
        out_ref[pl.ds(pl.multiple_of(theirs + c * size, 16), size), :] = done[c]
    for c in range(chunks):
        outward[c].wait_send()
        cross[c].wait_send()
        back[c].wait_send()


def head_sum(a, w, transposed, call_id):
    rows = a.shape[0]
    columns = w.shape[0] if transposed else w.shape[1]
    chunks = 3
    piece = (chunks, rows // 2 // chunks, columns)
    low = pltpu.VMEM(piece, jnp.bfloat16)
    return pl.pallas_call(
        functools.partial(head_sum_kernel, NT if transposed else NN, chunks),
        in_specs=[VMEM, VMEM],
        out_specs=VMEM,
        out_shape=jax.ShapeDtypeStruct((rows, columns), jnp.bfloat16),
        scratch_shapes=[
            low, low, pltpu.VMEM(piece, jnp.float32), low, low, low, low,
            pltpu.SemaphoreType.DMA((3, chunks)),
            pltpu.SemaphoreType.DMA((3, chunks)),
        ],
        compiler_params=pltpu.CompilerParams(
            collective_id=call_id, has_side_effects=True, vmem_limit_bytes=BIG
        ),
        cost_estimate=pl.CostEstimate(
            flops=2 * rows * columns * a.shape[1], bytes_accessed=40 * rows * columns, transcendentals=0
        ),
    )(a, w)


def swap(values):
    return lax.ppermute(values, "seq", [(0, 1), (1, 0)])


def gather_seq(values, axis):
    if lax.axis_size("seq") != 2:
        return lax.all_gather(values, "seq", axis=axis, tiled=True)
    other = swap(values)
    first = lax.axis_index("seq") == 0
    return jnp.concatenate(
        [jnp.where(first, values, other), jnp.where(first, other, values)], axis=axis
    )


def scatter_seq(values, axis):
    if lax.axis_size("seq") != 2:
        return lax.psum_scatter(
            values.astype(jnp.bfloat16), "seq", scatter_dimension=axis, tiled=True
        )
    size = values.shape[axis] // 2
    me = lax.axis_index("seq")
    kept = lax.dynamic_slice_in_dim(values, me * size, size, axis)
    sent = lax.dynamic_slice_in_dim(values, (1 - me) * size, size, axis)
    return (kept + swap(sent.astype(jnp.bfloat16)).astype(jnp.float32)).astype(jnp.bfloat16)


def own_part(values):
    size = values.shape[-1] // lax.axis_size("seq")
    return lax.dynamic_slice_in_dim(values, lax.axis_index("seq") * size, size, values.ndim - 1)


def on_device(
    frames, lengths, grad_out, w_qkv, qv_bias, w_out, w_up, up_bias, w_down, gains, shifts
):
    clip_count, rows_dev, model_width = frames.shape
    row_count = clip_count * rows_dev
    layers = w_qkv.shape[0]
    head_width = w_qkv.shape[3]
    query_scale = HD ** (-0.5)
    parts = lax.axis_size("seq")
    me = lax.axis_index("seq")
    key_length = rows_dev * parts
    positions = jnp.arange(key_length, dtype=jnp.int32)
    if parts == 2:
        positions = (positions + me * rows_dev) % key_length
    bias = jnp.where(positions < lengths[0], 0.0, -1e30).astype(jnp.float32)[:, None]

    vectors = gather_seq(jnp.concatenate([gains, shifts], axis=1), 2).astype(jnp.float32)
    gain_all, shift_all = vectors[:, :2], vectors[:, 2:]
    weights = []
    for l in range(layers):
        qkv = gather_seq(w_qkv[l], 1)
        weights.append(
            (
                qkv.transpose(1, 0, 2).reshape(model_width, 3 * head_width),
                gather_seq(w_out[l], 1),
                gather_seq(w_up[l], 0),
                gather_seq(w_down[l], 1),
            )
        )

    stream = frames.astype(jnp.float32).reshape(row_count, model_width)
    saved_layers = []
    for l in range(layers):
        qkv_full, out_full, up_full, down_full = weights[l]
        gain_pair, shift_set = gain_all[l], shift_all[l]
        bias_pair = qv_bias[l].astype(jnp.float32)
        normed = normalize(stream, gain_pair[0], shift_set[0]).astype(jnp.bfloat16)
        pair = jnp.dot(normed, qkv_full[:, head_width:], preferred_element_type=jnp.float32)
        pair = pair + jnp.concatenate([jnp.zeros_like(bias_pair[1]), bias_pair[1]])
        pair = pair.astype(jnp.bfloat16)
        if parts == 2:
            pair_all = jnp.concatenate([pair, swap(pair)], axis=0)
        else:
            pair_all = lax.all_gather(pair, "seq", axis=0, tiled=True)
        key_all, value_all = pair_all[:, :head_width], pair_all[:, head_width:]
        queries = jnp.dot(normed, qkv_full[:, :head_width], preferred_element_type=jnp.float32)
        queries = ((queries + bias_pair[0]) * query_scale).astype(jnp.bfloat16)
        attended, logsum = attend(queries, key_all, value_all, bias)
        mid = stream + head_sum(attended, out_full, False, 1).astype(jnp.float32) + shift_set[1]
        normed_two = normalize(mid, gain_pair[1], shift_set[2]).astype(jnp.bfloat16)
        hidden_pre = jnp.dot(normed_two, up_full, preferred_element_type=jnp.float32) + up_bias[
            l
        ].astype(jnp.float32)
        activated = gelu_exact(hidden_pre).astype(jnp.bfloat16)
        saved_layers.append(
            (stream, mid, normed, queries, key_all, value_all, logsum, attended, normed_two, hidden_pre, activated)
        )
        stream = (
            mid + head_sum(activated, down_full, False, 2).astype(jnp.float32) + shift_set[3]
        )
    output = stream.astype(jnp.bfloat16).reshape(clip_count, rows_dev, model_width)

    grad_stream = grad_out.astype(jnp.float32).reshape(row_count, model_width)
    owned = [None] * layers
    small = [None] * layers
    for l in range(layers - 1, -1, -1):
        (
            stream_in, mid, normed, queries, key_all, value_all,
            logsum, attended, normed_two, hidden_pre, activated,
        ) = saved_layers[l]
        qkv_full, out_full, up_full, down_full = weights[l]
        gain_pair, shift_set = gain_all[l], shift_all[l]
        grad_low = grad_stream.astype(jnp.bfloat16)
        d_shift_mlp = column_sum(grad_low)
        d_act = jnp.dot(grad_low, down_full.T, preferred_element_type=jnp.float32)
        gelu_value, gelu_pull = jax.vjp(gelu_exact, hidden_pre)
        d_hidden = gelu_pull(d_act)[0].astype(jnp.bfloat16)
        d_up_bias = column_sum(d_hidden)
        d_norm_two = head_sum(d_hidden, up_full, True, 3).astype(jnp.float32)
        share_down = scatter_seq(
            jnp.dot(activated.T, grad_low, preferred_element_type=jnp.float32), 1
        )
        share_up = scatter_seq(
            jnp.dot(normed_two.T, d_hidden, preferred_element_type=jnp.float32), 0
        )
        norm_value, norm_pull = jax.vjp(normalize, mid, gain_pair[1], shift_set[2])
        d_mid, d_gain_two, d_shift_two = norm_pull(d_norm_two)
        grad_stream = grad_stream + d_mid
        grad_low = grad_stream.astype(jnp.bfloat16)
        d_shift_attn = column_sum(grad_low)
        d_attended = jnp.dot(grad_low, out_full.T, preferred_element_type=jnp.float32).astype(
            jnp.bfloat16
        )
        d_query, d_key_part, d_value_part = attend_back(
            queries, key_all, value_all, bias, logsum, attended, d_attended
        )
        d_pair = jnp.concatenate([d_key_part, d_value_part], axis=1)
        if parts == 2:
            d_pair = (
                d_pair[:rows_dev].astype(jnp.float32) + swap(d_pair[rows_dev:]).astype(jnp.float32)
            ).astype(jnp.bfloat16)
        else:
            d_pair = lax.psum_scatter(d_pair, "seq", scatter_dimension=0, tiled=True)
        share_out = scatter_seq(
            jnp.dot(attended.T, grad_low, preferred_element_type=jnp.float32), 1
        )
        d_qkv = jnp.concatenate([d_query, d_pair], axis=1)
        d_normed = head_sum(d_qkv, qkv_full, True, 4).astype(jnp.float32)
        d_qkv_weight = jnp.dot(normed.T, d_qkv, preferred_element_type=jnp.float32)
        share_qkv = scatter_seq(d_qkv_weight, 0)
        share_qkv = share_qkv.reshape(-1, 3, head_width).transpose(1, 0, 2)
        d_bias = column_sum(d_qkv)
        norm_value, norm_pull = jax.vjp(normalize, stream_in, gain_pair[0], shift_set[0])
        d_before, d_gain_one, d_shift_one = norm_pull(d_normed)
        grad_stream = grad_stream + d_before
        owned[l] = (share_qkv, share_out, share_up, share_down)
        small[l] = (
            jnp.stack([d_bias[:head_width], d_bias[2 * head_width :]]),
            d_up_bias,
            jnp.stack([d_gain_one, d_gain_two]),
            jnp.stack([d_shift_one, d_shift_attn, d_shift_two, d_shift_mlp]),
        )
    owned = lax.psum(owned, "dp")
    grad_qkv, grad_out_weight, grad_up_weight, grad_down_weight = (
        stack_member(owned, p).astype(jnp.float32) for p in range(4)
    )
    grad_bias_pair, grad_bias_up, grad_gain_set, grad_shift_set = lax.psum(
        tuple(stack_member(small, p) for p in range(4)), ("dp", "seq")
    )
    grad_frames = grad_stream.reshape(clip_count, rows_dev, model_width)
    return (
        output,
        grad_frames,
        grad_qkv,
        grad_bias_pair,
        grad_out_weight,
        grad_up_weight,
        grad_bias_up,
        grad_down_weight,
        own_part(grad_gain_set),
        own_part(grad_shift_set),
    )


def solution(mesh):
    return jax.shard_map(
        on_device,
        mesh=mesh,
        in_specs=(
            P("dp", "seq", None),
            P("dp"),
            P("dp", "seq", None),
            P(None, None, "seq", "head"),
            P(None, None, "head"),
            P(None, "head", "seq"),
            P(None, "seq", "head"),
            P(None, "head"),
            P(None, "head", "seq"),
            P(None, None, "seq"),
            P(None, None, "seq"),
        ),
        out_specs=(
            P("dp", "seq", None),
            P("dp", "seq", None),
            P(None, None, "seq", "head"),
            P(None, None, "head"),
            P(None, "head", "seq"),
            P(None, "seq", "head"),
            P(None, "head"),
            P(None, "head", "seq"),
            P(None, None, "seq"),
            P(None, None, "seq"),
        ),
        check_vma=False,
    )
```

```python
import functools

import jax
import jax.numpy as jnp
from jax import lax
from jax.experimental import pallas as pl
from jax.experimental.pallas import tpu as pltpu
from jax.sharding import PartitionSpec as P

HD = 64


epsilon = 1e-05


def normalize(values, gain_vector, shift_vector):
    row_mean = jnp.mean(values, axis=-1, keepdims=True)
    centered = values - row_mean
    variance = jnp.mean(centered * centered, axis=-1, keepdims=True)
    return centered * lax.rsqrt(variance + epsilon) * gain_vector + shift_vector


def gelu_exact(values):
    return jax.nn.gelu(values, approximate=False)


def column_sum(values):
    return jnp.sum(values.astype(jnp.float32), axis=0)


def stack_member(collected, position):
    return jnp.stack([entry[position] for entry in collected])


NT = (((1,), (1,)), ((), ()))
NN = (((1,), (0,)), ((), ()))
VMEM = pl.BlockSpec(memory_space=pltpu.VMEM)
BIG = 48 * 1024 * 1024


def head_masks(shape, heads):
    column = lax.broadcasted_iota(jnp.int32, shape, 1)
    return [(column >= h * HD) & (column < (h + 1) * HD) for h in range(heads)]


def attend_kernel(heads, q_ref, k_ref, v_ref, bias_ref, out_ref, lse_ref, vt_ref):
    @pl.when(pl.program_id(0) == 0)
    def _():
        vt_ref[...] = v_ref[...].astype(jnp.float32).T.astype(jnp.bfloat16)

    queries = q_ref[...]
    zero = jnp.zeros_like(queries)
    parts = []
    for h, mask in enumerate(head_masks(queries.shape, heads)):
        scores = lax.dot_general(
            k_ref[...], jnp.where(mask, queries, zero), NT, preferred_element_type=jnp.float32
        )
        scores = scores + bias_ref[...]
        peak = jnp.max(scores, axis=0, keepdims=True)
        powered = jnp.exp(scores - peak)
        total = jnp.sum(powered, axis=0, keepdims=True)
        probs = (powered * (1.0 / total)).astype(jnp.bfloat16)
        parts.append(
            lax.dot_general(
                vt_ref[h * HD : (h + 1) * HD, :], probs, NN, preferred_element_type=jnp.float32
            )
        )
        lse_ref[0, h : h + 1, :] = peak + jnp.log(total)
    out_ref[...] = jnp.concatenate(parts, axis=0).T.astype(jnp.bfloat16)


def row_block(rows):
    return 256 if rows % 256 == 0 else rows


def attend(queries, key_all, value_all, bias):
    rows, width = queries.shape
    keys = key_all.shape[0]
    heads = width // HD
    block = row_block(rows)
    return pl.pallas_call(
        functools.partial(attend_kernel, heads),
        grid=(rows // block,),
        in_specs=[
            pl.BlockSpec((block, width), lambda i: (i, 0)),
            pl.BlockSpec((keys, width), lambda i: (0, 0)),
            pl.BlockSpec((keys, width), lambda i: (0, 0)),
            pl.BlockSpec((keys, 1), lambda i: (0, 0)),
        ],
        out_specs=[
            pl.BlockSpec((block, width), lambda i: (i, 0)),
            pl.BlockSpec((1, heads, block), lambda i: (i, 0, 0)),
        ],
        out_shape=[
            jax.ShapeDtypeStruct((rows, width), jnp.bfloat16),
            jax.ShapeDtypeStruct((rows // block, heads, block), jnp.float32),
        ],
        scratch_shapes=[pltpu.VMEM((width, keys), jnp.bfloat16)],
        compiler_params=pltpu.CompilerParams(vmem_limit_bytes=BIG),
        cost_estimate=pl.CostEstimate(
            flops=8 * rows * keys * width, bytes_accessed=6 * keys * width, transcendentals=rows * keys * heads
        ),
    )(queries, key_all, value_all, bias)


def attend_back_kernel(
    heads, q_ref, k_ref, v_ref, bias_ref, lse_ref, o_ref, do_ref, dq_ref, *rest
):
    *pair_refs, kt_ref, dk_sum, dv_sum = rest
    step = pl.program_id(0)

    @pl.when(step == 0)
    def _():
        kt_ref[...] = k_ref[...].astype(jnp.float32).T.astype(jnp.bfloat16)
        dk_sum[...] = jnp.zeros_like(dk_sum)
        dv_sum[...] = jnp.zeros_like(dv_sum)

    queries = q_ref[...]
    grads = do_ref[...]
    zero = jnp.zeros_like(queries)
    inner = (o_ref[...].astype(jnp.float32) * grads.astype(jnp.float32)).T
    parts = []
    for h, mask in enumerate(head_masks(queries.shape, heads)):
        q_head = jnp.where(mask, queries, zero)
        do_head = jnp.where(mask, grads, zero)
        delta = jnp.sum(inner[h * HD : (h + 1) * HD, :], axis=0, keepdims=True)
        scores = lax.dot_general(k_ref[...], q_head, NT, preferred_element_type=jnp.float32)
        probs = jnp.exp(scores + bias_ref[...] - lse_ref[0, h : h + 1, :])
        d_probs = lax.dot_general(v_ref[...], do_head, NT, preferred_element_type=jnp.float32)
        dv_sum[...] += jnp.dot(
            probs.astype(jnp.bfloat16), do_head, preferred_element_type=jnp.float32
        )
        d_scores = (probs * (d_probs - delta)).astype(jnp.bfloat16)
        dk_sum[...] += jnp.dot(d_scores, q_head, preferred_element_type=jnp.float32)
        parts.append(
            jnp.dot(
                kt_ref[h * HD : (h + 1) * HD, :], d_scores, preferred_element_type=jnp.float32
            )
        )
    d_query = jnp.concatenate(parts, axis=0).T.astype(jnp.bfloat16)
    dq_ref[...] = (d_query.astype(jnp.float32) * (HD ** (-0.5))).astype(jnp.bfloat16)

    @pl.when(step == pl.num_programs(0) - 1)
    def _():
        rows = pair_refs[0].shape[0]
        me = lax.axis_index("seq")
        starts = (me * rows, (1 - me) * rows) if len(pair_refs) == 2 else (0,)
        for start, pair_ref in zip(starts, pair_refs):
            place = pl.ds(pl.multiple_of(start, 16), rows)
            pair_ref[...] = jnp.concatenate(
                [dk_sum[place, :], dv_sum[place, :]], axis=1
            ).astype(jnp.bfloat16)


def attend_back(queries, key_all, value_all, bias, logsum, attended, d_attended, parts):
    rows, width = queries.shape
    keys = key_all.shape[0]
    heads = width // HD
    block = row_block(rows)
    row_spec = pl.BlockSpec((block, width), lambda i: (i, 0))
    key_spec = pl.BlockSpec((keys, width), lambda i: (0, 0))
    pieces = 2 if parts == 2 else 1
    pair = (keys // pieces, 2 * width)
    d_query, *d_pairs = pl.pallas_call(
        functools.partial(attend_back_kernel, heads),
        grid=(rows // block,),
        in_specs=[
            row_spec,
            key_spec,
            key_spec,
            pl.BlockSpec((keys, 1), lambda i: (0, 0)),
            pl.BlockSpec((1, heads, block), lambda i: (i, 0, 0)),
            row_spec,
            row_spec,
        ],
        out_specs=[row_spec] + [pl.BlockSpec(pair, lambda i: (0, 0))] * pieces,
        out_shape=[jax.ShapeDtypeStruct((rows, width), jnp.bfloat16)]
        + [jax.ShapeDtypeStruct(pair, jnp.bfloat16)] * pieces,
        scratch_shapes=[
            pltpu.VMEM((width, keys), jnp.bfloat16),
            pltpu.VMEM((keys, width), jnp.float32),
            pltpu.VMEM((keys, width), jnp.float32),
        ],
        compiler_params=pltpu.CompilerParams(vmem_limit_bytes=BIG),
        cost_estimate=pl.CostEstimate(
            flops=20 * rows * keys * width, bytes_accessed=12 * keys * width, transcendentals=rows * keys * heads
        ),
    )(queries, key_all, value_all, bias, logsum, attended, d_attended)
    return (d_query, d_pairs)


def head_sum_kernel(dims, chunks, a_ref, w_ref, out_ref, first, landed, own, chip, crossed, last, done, send, recv):
    me = lax.axis_index("head")
    core = me % 2
    sibling = me + 1 - 2 * core
    across = (me + 2) % 4
    half = a_ref.shape[0] // 2
    size = half // chunks
    mine = core * half
    theirs = (1 - core) * half

    barrier = pltpu.get_barrier_semaphore()
    for other in (sibling, across):
        pl.semaphore_signal(
            barrier, inc=1, device_id={"head": other}, device_id_type=pl.DeviceIdType.MESH
        )

    def product(base):
        rows = pl.ds(pl.multiple_of(base, 16), size)
        return lax.dot_general(a_ref[rows, :], w_ref[...], dims, preferred_element_type=jnp.float32)

    def remote(source, target, stage, c, other):
        return pltpu.make_async_remote_copy(
            src_ref=source.at[c],
            dst_ref=target.at[c],
            send_sem=send.at[stage, c],
            recv_sem=recv.at[stage, c],
            device_id={"head": other},
            device_id_type=pl.DeviceIdType.MESH,
        )

    outward = [remote(first, landed, 0, c, sibling) for c in range(chunks)]
    cross = [remote(chip, crossed, 1, c, across) for c in range(chunks)]
    back = [remote(last, done, 2, c, sibling) for c in range(chunks)]
    for c in range(chunks):
        first[c] = product(theirs + c * size).astype(jnp.bfloat16)
        if c == 0:
            pl.semaphore_wait(barrier, 2)
        outward[c].start()
    for c in range(chunks):
        own[c] = product(mine + c * size)
        outward[c].wait_recv()
        chip[c] = (own[c] + landed[c].astype(jnp.float32)).astype(jnp.bfloat16)
        cross[c].start()
    for c in range(chunks):
        cross[c].wait_recv()
        total = (chip[c].astype(jnp.float32) + crossed[c].astype(jnp.float32)).astype(jnp.bfloat16)
        last[c] = total
        back[c].start()
        out_ref[pl.ds(pl.multiple_of(mine + c * size, 16), size), :] = total
    for c in range(chunks):
        back[c].wait_recv()
        out_ref[pl.ds(pl.multiple_of(theirs + c * size, 16), size), :] = done[c]
    for c in range(chunks):
        outward[c].wait_send()
        cross[c].wait_send()
        back[c].wait_send()


def head_sum(a, w, transposed, call_id):
    rows = a.shape[0]
    columns = w.shape[0] if transposed else w.shape[1]
    chunks = 3
    piece = (chunks, rows // 2 // chunks, columns)
    low = pltpu.VMEM(piece, jnp.bfloat16)
    return pl.pallas_call(
        functools.partial(head_sum_kernel, NT if transposed else NN, chunks),
        in_specs=[VMEM, VMEM],
        out_specs=VMEM,
        out_shape=jax.ShapeDtypeStruct((rows, columns), jnp.bfloat16),
        scratch_shapes=[
            low, low, pltpu.VMEM(piece, jnp.float32), low, low, low, low,
            pltpu.SemaphoreType.DMA((3, chunks)),
            pltpu.SemaphoreType.DMA((3, chunks)),
        ],
        compiler_params=pltpu.CompilerParams(
            collective_id=call_id, has_side_effects=True, vmem_limit_bytes=BIG
        ),
        cost_estimate=pl.CostEstimate(
            flops=2 * rows * columns * a.shape[1], bytes_accessed=40 * rows * columns, transcendentals=0
        ),
    )(a, w)


def swap(values):
    return lax.ppermute(values, "seq", [(0, 1), (1, 0)])


def gather_seq(values, axis):
    if lax.axis_size("seq") != 2:
        return lax.all_gather(values, "seq", axis=axis, tiled=True)
    other = swap(values)
    first = lax.axis_index("seq") == 0
    return jnp.concatenate(
        [jnp.where(first, values, other), jnp.where(first, other, values)], axis=axis
    )


def after(earlier, *values):
    return lax.optimization_barrier((earlier, *values))[1:]


def scatter_seq(values):
    if lax.axis_size("seq") != 2:
        return (None, values.astype(jnp.bfloat16))
    size = values.shape[1] // 2
    me = lax.axis_index("seq")
    kept = lax.dynamic_slice_in_dim(values, me * size, size, 1)
    sent = lax.dynamic_slice_in_dim(values, (1 - me) * size, size, 1)
    return (kept, sent.astype(jnp.bfloat16))


def finish_seq(kept, sent):
    if lax.axis_size("seq") != 2:
        return lax.psum_scatter(sent, "seq", scatter_dimension=1, tiled=True)
    return (kept.astype(jnp.float32) + swap(sent).astype(jnp.float32)).astype(jnp.bfloat16)


def shifted(values, axis, shift):
    n = lax.axis_size(axis)
    return lax.ppermute(values, axis, [(i, (i + shift) % n) for i in range(n)])


def sum_dp(values):
    n = lax.axis_size("dp")
    me = lax.axis_index("dp")
    size = values.shape[0] // n

    def share(shift):
        return lax.dynamic_slice_in_dim(values, (me + shift) % n * size, size, 0)

    total = share(0).astype(jnp.float32)
    for shift in range(1, n):
        total = total + shifted(share(shift), "dp", shift).astype(jnp.float32)
    total = total.astype(jnp.bfloat16)
    result = jnp.zeros(values.shape, jnp.bfloat16)
    result = lax.dynamic_update_slice_in_dim(result, total, me * size, 0)
    for shift in range(1, n):
        result = lax.dynamic_update_slice_in_dim(
            result, shifted(total, "dp", shift), (me + n - shift) % n * size, 0
        )
    return result


def sum_pairwise(values, axis):
    n = lax.axis_size(axis)
    step = 1
    while step < n:
        values = values + lax.ppermute(values, axis, [(i, i ^ step) for i in range(n)])
        step *= 2
    return values


def own_part(values):
    size = values.shape[-1] // lax.axis_size("seq")
    return lax.dynamic_slice_in_dim(values, lax.axis_index("seq") * size, size, values.ndim - 1)


def cross(left, right):
    return lax.dot_general(
        left, right, (((0,), (0,)), ((), ())), preferred_element_type=jnp.float32
    )


def on_device(
    frames, lengths, grad_out, w_qkv, qv_bias, w_out, w_up, up_bias, w_down, gains, shifts
):
    clip_count, rows_dev, model_width = frames.shape
    row_count = clip_count * rows_dev
    layers = w_qkv.shape[0]
    head_width = w_qkv.shape[3]
    units = w_up.shape[2]
    query_scale = HD ** (-0.5)
    parts = lax.axis_size("seq")
    key_length = rows_dev * parts
    positions = jnp.arange(key_length, dtype=jnp.int32)
    bias = jnp.where(positions < lengths[0], 0.0, -1e30).astype(jnp.float32)[:, None]

    vectors = jnp.concatenate([gains, shifts], axis=1)
    vectors = lax.all_gather(vectors, "seq", axis=2, tiled=True).astype(jnp.float32)
    gain_all, shift_all = vectors[:, :2], vectors[:, 2:]
    flat_qkv = w_qkv.transpose(0, 2, 1, 3).reshape(layers, -1, 3 * head_width)
    qkv_full = lax.all_gather(flat_qkv[0], "seq", axis=0, tiled=True)

    stream = frames.astype(jnp.float32).reshape(row_count, model_width)
    saved_layers = []
    weights = []
    next_weights = None
    for l in range(layers):
        gain_pair, shift_set = gain_all[l], shift_all[l]
        bias_pair = qv_bias[l].astype(jnp.float32)
        if l > 0:
            qkv_full, out_full, up_full, down_full = next_weights
        normed = normalize(stream, gain_pair[0], shift_set[0]).astype(jnp.bfloat16)
        pair = jnp.dot(normed, qkv_full[:, head_width:], preferred_element_type=jnp.float32)
        pair = pair + jnp.concatenate([jnp.zeros_like(bias_pair[1]), bias_pair[1]])
        pair_all = lax.all_gather(pair.astype(jnp.bfloat16), "seq", axis=0, tiled=True)
        if l == 0:
            own = after(pair_all, w_out[0], w_up[0], w_down[0])
            out_full = gather_seq(own[0], 1)
            own = after(out_full, own[1])
            up_full = gather_seq(own[0], 0)
            down_full = gather_seq(after(up_full, w_down[0])[0], 1)
        key_all, value_all = pair_all[:, :head_width], pair_all[:, head_width:]
        queries = jnp.dot(normed, qkv_full[:, :head_width], preferred_element_type=jnp.float32)
        queries = ((queries + bias_pair[0]) * query_scale).astype(jnp.bfloat16)
        attended, logsum = attend(queries, key_all, value_all, bias)
        mid = stream + head_sum(attended, out_full, False, 1).astype(jnp.float32) + shift_set[1]
        normed_two = normalize(mid, gain_pair[1], shift_set[2]).astype(jnp.bfloat16)
        weights.append((qkv_full, out_full, up_full, down_full))
        if l + 1 < layers:
            own = after(normed_two, flat_qkv[l + 1], w_out[l + 1], w_up[l + 1], w_down[l + 1])
            next_weights = tuple(gather_seq(w, axis) for w, axis in zip(own, (0, 1, 0, 1)))
        hidden_pre = jnp.dot(normed_two, up_full, preferred_element_type=jnp.float32) + up_bias[
            l
        ].astype(jnp.float32)
        activated = gelu_exact(hidden_pre).astype(jnp.bfloat16)
        saved_layers.append(
            (stream, mid, normed, queries, key_all, value_all, logsum, attended, normed_two, hidden_pre, activated)
        )
        stream = (
            mid + head_sum(activated, down_full, False, 2).astype(jnp.float32) + shift_set[3]
        )
    output = stream.astype(jnp.bfloat16).reshape(clip_count, rows_dev, model_width)

    grad_stream = grad_out.astype(jnp.float32).reshape(row_count, model_width)
    owned = [None] * layers
    small = [None] * layers
    for l in range(layers - 1, -1, -1):
        (
            stream_in, mid, normed, queries, key_all, value_all,
            logsum, attended, normed_two, hidden_pre, activated,
        ) = saved_layers[l]
        qkv_full, out_full, up_full, down_full = weights[l]
        gain_pair, shift_set = gain_all[l], shift_all[l]
        grad_low = grad_stream.astype(jnp.bfloat16)
        d_shift_mlp = column_sum(grad_low)
        d_act = jnp.dot(grad_low, down_full.T, preferred_element_type=jnp.float32)
        gelu_value, gelu_pull = jax.vjp(gelu_exact, hidden_pre)
        d_hidden = gelu_pull(d_act)[0].astype(jnp.bfloat16)
        d_up_bias = column_sum(d_hidden)
        kept, sent = scatter_seq(
            jnp.concatenate([cross(activated, grad_low), cross(d_hidden, normed_two)], axis=0)
        )
        d_hidden, sent = lax.optimization_barrier((d_hidden, sent))
        share_mlp = finish_seq(kept, sent)
        d_norm_two = head_sum(d_hidden, up_full, True, 3).astype(jnp.float32)
        norm_value, norm_pull = jax.vjp(normalize, mid, gain_pair[1], shift_set[2])
        d_mid, d_gain_two, d_shift_two = norm_pull(d_norm_two)
        grad_stream = grad_stream + d_mid
        grad_low = grad_stream.astype(jnp.bfloat16)
        d_shift_attn = column_sum(grad_low)
        d_attended = jnp.dot(grad_low, out_full.T, preferred_element_type=jnp.float32).astype(
            jnp.bfloat16
        )
        d_query, d_pairs = attend_back(
            queries, key_all, value_all, bias, logsum, attended, d_attended, parts
        )
        if parts == 2:
            d_pair = (
                d_pairs[0].astype(jnp.float32) + swap(d_pairs[1]).astype(jnp.float32)
            ).astype(jnp.bfloat16)
        else:
            d_pair = lax.psum_scatter(d_pairs[0], "seq", scatter_dimension=0, tiled=True)
        d_qkv = jnp.concatenate([d_query, d_pair], axis=1)
        kept, sent = scatter_seq(
            jnp.concatenate([cross(d_qkv, normed), cross(attended, grad_low)], axis=0)
        )
        d_qkv, sent = lax.optimization_barrier((d_qkv, sent))
        share_attn = finish_seq(kept, sent)
        d_normed = head_sum(d_qkv, qkv_full, True, 4).astype(jnp.float32)
        d_bias = column_sum(d_qkv)
        norm_value, norm_pull = jax.vjp(normalize, stream_in, gain_pair[0], shift_set[0])
        d_before, d_gain_one, d_shift_one = norm_pull(d_normed)
        grad_stream = grad_stream + d_before
        owned[l] = (sum_dp(share_mlp), sum_dp(share_attn))
        small[l] = [
            d_gain_one, d_gain_two, d_shift_one, d_shift_attn, d_shift_two, d_shift_mlp,
            d_up_bias, d_bias[:head_width], d_bias[2 * head_width :],
        ]
    vector_sums = jnp.concatenate([v for entry in small for v in entry]).reshape(-1, 128)
    vector_sums = sum_pairwise(sum_pairwise(vector_sums, "seq"), "dp").reshape(layers, -1)
    d = model_width
    grad_gain_set = vector_sums[:, : 2 * d].reshape(layers, 2, d)
    grad_shift_set = vector_sums[:, 2 * d : 6 * d].reshape(layers, 4, d)
    grad_bias_up = vector_sums[:, 6 * d : 6 * d + units]
    grad_bias_pair = vector_sums[:, 6 * d + units :].reshape(layers, 2, head_width)

    mlp = [entry[0].astype(jnp.float32) for entry in owned]
    attn = [entry[1].astype(jnp.float32) for entry in owned]
    grad_down_weight = jnp.stack([m[:units] for m in mlp])
    grad_up_weight = jnp.stack([m[units:].T for m in mlp])
    grad_qkv = jnp.stack(
        [m[: 3 * head_width].reshape(3, head_width, -1).transpose(0, 2, 1) for m in attn]
    )
    grad_out_weight = jnp.stack([m[3 * head_width :] for m in attn])
    grad_frames = grad_stream.reshape(clip_count, rows_dev, model_width)
    return (
        output,
        grad_frames,
        grad_qkv,
        grad_bias_pair,
        grad_out_weight,
        grad_up_weight,
        grad_bias_up,
        grad_down_weight,
        own_part(grad_gain_set),
        own_part(grad_shift_set),
    )


def solution(mesh):
    return jax.shard_map(
        on_device,
        mesh=mesh,
        in_specs=(
            P("dp", "seq", None),
            P("dp"),
            P("dp", "seq", None),
            P(None, None, "seq", "head"),
            P(None, None, "head"),
            P(None, "head", "seq"),
            P(None, "seq", "head"),
            P(None, "head"),
            P(None, "head", "seq"),
            P(None, None, "seq"),
            P(None, None, "seq"),
        ),
        out_specs=(
            P("dp", "seq", None),
            P("dp", "seq", None),
            P(None, None, "seq", "head"),
            P(None, None, "head"),
            P(None, "head", "seq"),
            P(None, "seq", "head"),
            P(None, "head"),
            P(None, "head", "seq"),
            P(None, None, "seq"),
            P(None, None, "seq"),
        ),
        check_vma=False,
    )
```

```python
import functools

import jax
import jax.numpy as jnp
from jax import lax
from jax.experimental import pallas as pl
from jax.experimental.pallas import tpu as pltpu
from jax.sharding import PartitionSpec as P

HD = 64


epsilon = 1e-05


def normalize(values, gain_vector, shift_vector):
    row_mean = jnp.mean(values, axis=-1, keepdims=True)
    centered = values - row_mean
    variance = jnp.mean(centered * centered, axis=-1, keepdims=True)
    return centered * lax.rsqrt(variance + epsilon) * gain_vector + shift_vector


def gelu_exact(values):
    return jax.nn.gelu(values, approximate=False)


def column_sum(values):
    return jnp.sum(values.astype(jnp.float32), axis=0)


def stack_member(collected, position):
    return jnp.stack([entry[position] for entry in collected])


NT = (((1,), (1,)), ((), ()))
NN = (((1,), (0,)), ((), ()))
VMEM = pl.BlockSpec(memory_space=pltpu.VMEM)
BIG = 48 * 1024 * 1024


def head_masks(shape, heads):
    column = lax.broadcasted_iota(jnp.int32, shape, 1)
    return [(column >= h * HD) & (column < (h + 1) * HD) for h in range(heads)]


def attend_kernel(heads, q_ref, k_ref, v_ref, bias_ref, out_ref, lse_ref, vt_ref):
    @pl.when(pl.program_id(0) == 0)
    def _():
        vt_ref[...] = v_ref[...].astype(jnp.float32).T.astype(jnp.bfloat16)

    queries = q_ref[...]
    zero = jnp.zeros_like(queries)
    parts = []
    for h, mask in enumerate(head_masks(queries.shape, heads)):
        scores = lax.dot_general(
            k_ref[...], jnp.where(mask, queries, zero), NT, preferred_element_type=jnp.float32
        )
        scores = scores + bias_ref[...]
        peak = jnp.max(scores, axis=0, keepdims=True)
        powered = jnp.exp(scores - peak)
        total = jnp.sum(powered, axis=0, keepdims=True)
        probs = (powered * (1.0 / total)).astype(jnp.bfloat16)
        parts.append(
            lax.dot_general(
                vt_ref[h * HD : (h + 1) * HD, :], probs, NN, preferred_element_type=jnp.float32
            )
        )
        lse_ref[0, h : h + 1, :] = peak + jnp.log(total)
    out_ref[...] = jnp.concatenate(parts, axis=0).T.astype(jnp.bfloat16)


def row_block(rows):
    return 256 if rows % 256 == 0 else rows


def attend(queries, key_all, value_all, bias):
    rows, width = queries.shape
    keys = key_all.shape[0]
    heads = width // HD
    block = row_block(rows)
    return pl.pallas_call(
        functools.partial(attend_kernel, heads),
        grid=(rows // block,),
        in_specs=[
            pl.BlockSpec((block, width), lambda i: (i, 0)),
            pl.BlockSpec((keys, width), lambda i: (0, 0)),
            pl.BlockSpec((keys, width), lambda i: (0, 0)),
            pl.BlockSpec((keys, 1), lambda i: (0, 0)),
        ],
        out_specs=[
            pl.BlockSpec((block, width), lambda i: (i, 0)),
            pl.BlockSpec((1, heads, block), lambda i: (i, 0, 0)),
        ],
        out_shape=[
            jax.ShapeDtypeStruct((rows, width), jnp.bfloat16),
            jax.ShapeDtypeStruct((rows // block, heads, block), jnp.float32),
        ],
        scratch_shapes=[pltpu.VMEM((width, keys), jnp.bfloat16)],
        compiler_params=pltpu.CompilerParams(vmem_limit_bytes=BIG),
        cost_estimate=pl.CostEstimate(flops=1024, bytes_accessed=1024, transcendentals=0
        ),
    )(queries, key_all, value_all, bias)


def attend_back_kernel(
    heads, q_ref, k_ref, v_ref, bias_ref, lse_ref, o_ref, do_ref, dq_ref, *rest
):
    *pair_refs, kt_ref, dk_sum, dv_sum = rest
    step = pl.program_id(0)

    @pl.when(step == 0)
    def _():
        kt_ref[...] = k_ref[...].astype(jnp.float32).T.astype(jnp.bfloat16)
        dk_sum[...] = jnp.zeros_like(dk_sum)
        dv_sum[...] = jnp.zeros_like(dv_sum)

    queries = q_ref[...]
    grads = do_ref[...]
    zero = jnp.zeros_like(queries)
    inner = (o_ref[...].astype(jnp.float32) * grads.astype(jnp.float32)).T
    parts = []
    for h, mask in enumerate(head_masks(queries.shape, heads)):
        q_head = jnp.where(mask, queries, zero)
        do_head = jnp.where(mask, grads, zero)
        delta = jnp.sum(inner[h * HD : (h + 1) * HD, :], axis=0, keepdims=True)
        scores = lax.dot_general(k_ref[...], q_head, NT, preferred_element_type=jnp.float32)
        probs = jnp.exp(scores + bias_ref[...] - lse_ref[0, h : h + 1, :])
        d_probs = lax.dot_general(v_ref[...], do_head, NT, preferred_element_type=jnp.float32)
        dv_sum[...] += jnp.dot(
            probs.astype(jnp.bfloat16), do_head, preferred_element_type=jnp.float32
        )
        d_scores = (probs * (d_probs - delta)).astype(jnp.bfloat16)
        dk_sum[...] += jnp.dot(d_scores, q_head, preferred_element_type=jnp.float32)
        parts.append(
            jnp.dot(
                kt_ref[h * HD : (h + 1) * HD, :], d_scores, preferred_element_type=jnp.float32
            )
        )
    d_query = jnp.concatenate(parts, axis=0).T.astype(jnp.bfloat16)
    dq_ref[...] = (d_query.astype(jnp.float32) * (HD ** (-0.5))).astype(jnp.bfloat16)

    @pl.when(step == pl.num_programs(0) - 1)
    def _():
        rows = pair_refs[0].shape[0]
        me = lax.axis_index("seq")
        starts = (me * rows, (1 - me) * rows) if len(pair_refs) == 2 else (0,)
        for start, pair_ref in zip(starts, pair_refs):
            place = pl.ds(pl.multiple_of(start, 16), rows)
            pair_ref[...] = jnp.concatenate(
                [dk_sum[place, :], dv_sum[place, :]], axis=1
            ).astype(jnp.bfloat16)


def attend_back(queries, key_all, value_all, bias, logsum, attended, d_attended, parts):
    rows, width = queries.shape
    keys = key_all.shape[0]
    heads = width // HD
    block = row_block(rows)
    row_spec = pl.BlockSpec((block, width), lambda i: (i, 0))
    key_spec = pl.BlockSpec((keys, width), lambda i: (0, 0))
    pieces = 2 if parts == 2 else 1
    pair = (keys // pieces, 2 * width)
    d_query, *d_pairs = pl.pallas_call(
        functools.partial(attend_back_kernel, heads),
        grid=(rows // block,),
        in_specs=[
            row_spec,
            key_spec,
            key_spec,
            pl.BlockSpec((keys, 1), lambda i: (0, 0)),
            pl.BlockSpec((1, heads, block), lambda i: (i, 0, 0)),
            row_spec,
            row_spec,
        ],
        out_specs=[row_spec] + [pl.BlockSpec(pair, lambda i: (0, 0))] * pieces,
        out_shape=[jax.ShapeDtypeStruct((rows, width), jnp.bfloat16)]
        + [jax.ShapeDtypeStruct(pair, jnp.bfloat16)] * pieces,
        scratch_shapes=[
            pltpu.VMEM((width, keys), jnp.bfloat16),
            pltpu.VMEM((keys, width), jnp.float32),
            pltpu.VMEM((keys, width), jnp.float32),
        ],
        compiler_params=pltpu.CompilerParams(vmem_limit_bytes=BIG),
        cost_estimate=pl.CostEstimate(flops=1024, bytes_accessed=1024, transcendentals=0
        ),
    )(queries, key_all, value_all, bias, logsum, attended, d_attended)
    return (d_query, d_pairs)


def head_sum_kernel(dims, chunks, carries, *refs):
    if carries:
        a_ref, w_ref, sent_ref, out_ref, got_ref, *refs, carry_send, carry_recv = refs
    else:
        a_ref, w_ref, out_ref, *refs = refs
    first, landed, own, chip, crossed, last, done, send, recv = refs
    me = lax.axis_index("head")
    core = me % 2
    sibling = me + 1 - 2 * core
    across = (me + 2) % 4
    half = a_ref.shape[0] // 2
    size = half // chunks
    mine = core * half
    theirs = (1 - core) * half

    barrier = pltpu.get_barrier_semaphore()
    for other in (sibling, across):
        pl.semaphore_signal(
            barrier, inc=1, device_id={"head": other}, device_id_type=pl.DeviceIdType.MESH
        )

    if carries:
        facing = 1 - lax.axis_index("seq")
        pl.semaphore_signal(
            barrier, inc=1, device_id={"seq": facing}, device_id_type=pl.DeviceIdType.MESH
        )
        carry = pltpu.make_async_remote_copy(
            src_ref=sent_ref,
            dst_ref=got_ref,
            send_sem=carry_send,
            recv_sem=carry_recv,
            device_id={"seq": facing},
            device_id_type=pl.DeviceIdType.MESH,
        )

    def product(base):
        rows = pl.ds(pl.multiple_of(base, 16), size)
        return lax.dot_general(a_ref[rows, :], w_ref[...], dims, preferred_element_type=jnp.float32)

    def remote(source, target, stage, c, other):
        return pltpu.make_async_remote_copy(
            src_ref=source.at[c],
            dst_ref=target.at[c],
            send_sem=send.at[stage, c],
            recv_sem=recv.at[stage, c],
            device_id={"head": other},
            device_id_type=pl.DeviceIdType.MESH,
        )

    outward = [remote(first, landed, 0, c, sibling) for c in range(chunks)]
    cross = [remote(chip, crossed, 1, c, across) for c in range(chunks)]
    back = [remote(last, done, 2, c, sibling) for c in range(chunks)]
    ahead = 2

    def offer(c):
        first[c] = product(theirs + c * size).astype(jnp.bfloat16)
        if c == 0:
            pl.semaphore_wait(barrier, 3 if carries else 2)
            if carries:
                carry.start()
        outward[c].start()

    for c in range(ahead):
        offer(c)
    for c in range(chunks):
        own[c] = product(mine + c * size)
        if c + ahead < chunks:
            offer(c + ahead)
        outward[c].wait_recv()
        chip[c] = (own[c] + landed[c].astype(jnp.float32)).astype(jnp.bfloat16)
        cross[c].start()
    for c in range(chunks):
        cross[c].wait_recv()
        total = (chip[c].astype(jnp.float32) + crossed[c].astype(jnp.float32)).astype(jnp.bfloat16)
        last[c] = total
        back[c].start()
        out_ref[pl.ds(pl.multiple_of(mine + c * size, 16), size), :] = total
    for c in range(chunks):
        back[c].wait_recv()
        out_ref[pl.ds(pl.multiple_of(theirs + c * size, 16), size), :] = done[c]
    for c in range(chunks):
        outward[c].wait_send()
        cross[c].wait_send()
        back[c].wait_send()
    if carries:
        carry.wait()


def head_sum(a, w, transposed, call_id, sent=None):
    rows = a.shape[0]
    columns = w.shape[0] if transposed else w.shape[1]
    chunks = 6
    carries = sent is not None
    piece = (chunks, rows // 2 // chunks, columns)
    low = pltpu.VMEM(piece, jnp.bfloat16)
    out_shape = [jax.ShapeDtypeStruct((rows, columns), jnp.bfloat16)]
    scratch = [
        low, low, pltpu.VMEM(piece, jnp.float32), low, low, low, low,
        pltpu.SemaphoreType.DMA((3, chunks)),
        pltpu.SemaphoreType.DMA((3, chunks)),
    ]
    anywhere = [pl.BlockSpec(memory_space=pl.ANY)] if carries else []
    if carries:
        out_shape.append(jax.ShapeDtypeStruct(sent.shape, sent.dtype))
        scratch += [pltpu.SemaphoreType.DMA, pltpu.SemaphoreType.DMA]
    result = pl.pallas_call(
        functools.partial(head_sum_kernel, NT if transposed else NN, chunks, carries),
        in_specs=[VMEM, VMEM] + anywhere,
        out_specs=[VMEM] + anywhere,
        out_shape=out_shape,
        scratch_shapes=scratch,
        compiler_params=pltpu.CompilerParams(
            collective_id=call_id, has_side_effects=True, vmem_limit_bytes=BIG
        ),
        cost_estimate=pl.CostEstimate(flops=1024, bytes_accessed=1024, transcendentals=0),
    )(a, w, *([sent] if carries else []))
    return result if carries else result[0]


def head_sum_and_seq(a, w, call_id, values):
    if lax.axis_size("seq") != 2:
        shares = lax.psum_scatter(
            values.astype(jnp.bfloat16), "seq", scatter_dimension=1, tiled=True
        )
        return (head_sum(a, w, True, call_id), shares)
    size = values.shape[1] // 2
    me = lax.axis_index("seq")
    kept = lax.dynamic_slice_in_dim(values, me * size, size, 1)
    sent = lax.dynamic_slice_in_dim(values, (1 - me) * size, size, 1).astype(jnp.bfloat16)
    total, got = head_sum(a, w, True, call_id, sent)
    return (total, (kept + got.astype(jnp.float32)).astype(jnp.bfloat16))


def swap(values):
    return lax.ppermute(values, "seq", [(0, 1), (1, 0)])


def gather_seq(values, axis):
    if lax.axis_size("seq") != 2:
        return lax.all_gather(values, "seq", axis=axis, tiled=True)
    other = swap(values)
    first = lax.axis_index("seq") == 0
    return jnp.concatenate(
        [jnp.where(first, values, other), jnp.where(first, other, values)], axis=axis
    )


def after(earlier, *values):
    return lax.optimization_barrier((earlier, *values))[1:]


def sum_pairwise(values, axis):
    n = lax.axis_size(axis)
    step = 1
    while step < n:
        values = values + lax.ppermute(values, axis, [(i, i ^ step) for i in range(n)])
        step *= 2
    return values


def own_part(values):
    size = values.shape[-1] // lax.axis_size("seq")
    return lax.dynamic_slice_in_dim(values, lax.axis_index("seq") * size, size, values.ndim - 1)


def cross(left, right):
    return lax.dot_general(
        left, right, (((0,), (0,)), ((), ())), preferred_element_type=jnp.float32
    )


def on_device(
    frames, lengths, grad_out, w_qkv, qv_bias, w_out, w_up, up_bias, w_down, gains, shifts
):
    clip_count, rows_dev, model_width = frames.shape
    row_count = clip_count * rows_dev
    layers = w_qkv.shape[0]
    head_width = w_qkv.shape[3]
    units = w_up.shape[2]
    query_scale = HD ** (-0.5)
    parts = lax.axis_size("seq")
    key_length = rows_dev * parts
    positions = jnp.arange(key_length, dtype=jnp.int32)
    bias = jnp.where(positions < lengths[0], 0.0, -1e30).astype(jnp.float32)[:, None]

    vectors = jnp.concatenate([gains, shifts], axis=1)
    vectors = lax.all_gather(vectors, "seq", axis=2, tiled=True).astype(jnp.float32)
    gain_all, shift_all = vectors[:, :2], vectors[:, 2:]
    flat_qkv = w_qkv.transpose(0, 2, 1, 3).reshape(layers, -1, 3 * head_width)
    qkv_full = lax.all_gather(flat_qkv[0], "seq", axis=0, tiled=True)
    own = after(qkv_full, w_out[0], w_up[0], w_down[0])
    out_full, up_full, down_full = (gather_seq(w, axis) for w, axis in zip(own, (1, 0, 1)))

    stream = frames.astype(jnp.float32).reshape(row_count, model_width)
    saved_layers = []
    weights = []
    next_weights = None
    for l in range(layers):
        gain_pair, shift_set = gain_all[l], shift_all[l]
        bias_pair = qv_bias[l].astype(jnp.float32)
        if l > 0:
            qkv_full, out_full, up_full, down_full = next_weights
        normed = normalize(stream, gain_pair[0], shift_set[0]).astype(jnp.bfloat16)
        pair = jnp.dot(normed, qkv_full[:, head_width:], preferred_element_type=jnp.float32)
        pair = pair + jnp.concatenate([jnp.zeros_like(bias_pair[1]), bias_pair[1]])
        pair_all = lax.all_gather(pair.astype(jnp.bfloat16), "seq", axis=0, tiled=True)
        key_all, value_all = pair_all[:, :head_width], pair_all[:, head_width:]
        queries = jnp.dot(normed, qkv_full[:, :head_width], preferred_element_type=jnp.float32)
        queries = ((queries + bias_pair[0]) * query_scale).astype(jnp.bfloat16)
        attended, logsum = attend(queries, key_all, value_all, bias)
        mid = stream + head_sum(attended, out_full, False, 1).astype(jnp.float32) + shift_set[1]
        normed_two = normalize(mid, gain_pair[1], shift_set[2]).astype(jnp.bfloat16)
        weights.append((qkv_full, out_full, up_full, down_full))
        if l + 1 < layers:
            own = after(attended, flat_qkv[l + 1], w_out[l + 1], w_up[l + 1], w_down[l + 1])
            next_weights = tuple(gather_seq(w, axis) for w, axis in zip(own, (0, 1, 0, 1)))
        hidden_pre = jnp.dot(normed_two, up_full, preferred_element_type=jnp.float32) + up_bias[
            l
        ].astype(jnp.float32)
        activated = gelu_exact(hidden_pre).astype(jnp.bfloat16)
        saved_layers.append(
            (stream, mid, normed, queries, key_all, value_all, logsum, attended, normed_two, hidden_pre, activated)
        )
        stream = (
            mid + head_sum(activated, down_full, False, 2).astype(jnp.float32) + shift_set[3]
        )
    output = stream.astype(jnp.bfloat16).reshape(clip_count, rows_dev, model_width)

    grad_stream = grad_out.astype(jnp.float32).reshape(row_count, model_width)
    owned = [None] * layers
    small = [None] * layers
    for l in range(layers - 1, -1, -1):
        (
            stream_in, mid, normed, queries, key_all, value_all,
            logsum, attended, normed_two, hidden_pre, activated,
        ) = saved_layers[l]
        qkv_full, out_full, up_full, down_full = weights[l]
        gain_pair, shift_set = gain_all[l], shift_all[l]
        grad_low = grad_stream.astype(jnp.bfloat16)
        d_shift_mlp = column_sum(grad_low)
        d_act = jnp.dot(grad_low, down_full.T, preferred_element_type=jnp.float32)
        gelu_value, gelu_pull = jax.vjp(gelu_exact, hidden_pre)
        d_hidden = gelu_pull(d_act)[0].astype(jnp.bfloat16)
        d_up_bias = column_sum(d_hidden)
        mlp_grads = jnp.concatenate(
            [cross(activated, grad_low), cross(d_hidden, normed_two)], axis=0
        )
        if l + 1 < layers:
            d_hidden, packed = lax.optimization_barrier((d_hidden, packed))
            owned[l + 1] = lax.psum(packed, "dp")
        d_norm_two, share_mlp = head_sum_and_seq(d_hidden, up_full, 3, mlp_grads)
        d_norm_two = d_norm_two.astype(jnp.float32)
        norm_value, norm_pull = jax.vjp(normalize, mid, gain_pair[1], shift_set[2])
        d_mid, d_gain_two, d_shift_two = norm_pull(d_norm_two)
        grad_stream = grad_stream + d_mid
        grad_low = grad_stream.astype(jnp.bfloat16)
        d_shift_attn = column_sum(grad_low)
        d_attended = jnp.dot(grad_low, out_full.T, preferred_element_type=jnp.float32).astype(
            jnp.bfloat16
        )
        d_query, d_pairs = attend_back(
            queries, key_all, value_all, bias, logsum, attended, d_attended, parts
        )
        if parts == 2:
            d_pair = (
                d_pairs[0].astype(jnp.float32) + swap(d_pairs[1]).astype(jnp.float32)
            ).astype(jnp.bfloat16)
        else:
            d_pair = lax.psum_scatter(d_pairs[0], "seq", scatter_dimension=0, tiled=True)
        d_qkv = jnp.concatenate([d_query, d_pair], axis=1)
        attn_grads = jnp.concatenate([cross(d_qkv, normed), cross(attended, grad_low)], axis=0)
        if l + 1 < layers:
            d_qkv, share_mlp, owned[l + 1] = lax.optimization_barrier(
                (d_qkv, share_mlp, owned[l + 1])
            )
        d_normed, share_attn = head_sum_and_seq(d_qkv, qkv_full, 4, attn_grads)
        d_normed = d_normed.astype(jnp.float32)
        d_bias = column_sum(d_qkv)
        norm_value, norm_pull = jax.vjp(normalize, stream_in, gain_pair[0], shift_set[0])
        d_before, d_gain_one, d_shift_one = norm_pull(d_normed)
        grad_stream = grad_stream + d_before
        if l > 0:
            packed = jnp.concatenate([share_mlp, share_attn], axis=0)
        else:
            owned_mlp = lax.psum(share_mlp, "dp")
            owned_mlp, share_attn = lax.optimization_barrier((owned_mlp, share_attn))
            owned[l] = (owned_mlp, lax.psum(share_attn, "dp"))
        small[l] = [
            d_gain_one, d_gain_two, d_shift_one, d_shift_attn, d_shift_two, d_shift_mlp,
            d_up_bias, d_bias[:head_width], d_bias[2 * head_width :],
        ]
    vector_sums = jnp.concatenate([v for entry in small for v in entry]).reshape(-1, 128)
    vector_sums = sum_pairwise(sum_pairwise(vector_sums, "seq"), "dp").reshape(layers, -1)
    d = model_width
    grad_gain_set = vector_sums[:, : 2 * d].reshape(layers, 2, d)
    grad_shift_set = vector_sums[:, 2 * d : 6 * d].reshape(layers, 4, d)
    grad_bias_up = vector_sums[:, 6 * d : 6 * d + units]
    grad_bias_pair = vector_sums[:, 6 * d + units :].reshape(layers, 2, head_width)

    mlp, attn = [owned[0][0].astype(jnp.float32)], [owned[0][1].astype(jnp.float32)]
    for entry in owned[1:]:
        mlp.append(entry[: 2 * units].astype(jnp.float32))
        attn.append(entry[2 * units :].astype(jnp.float32))
    grad_down_weight = jnp.stack([m[:units] for m in mlp])
    grad_up_weight = jnp.stack([m[units:].T for m in mlp])
    grad_qkv = jnp.stack(
        [m[: 3 * head_width].reshape(3, head_width, -1).transpose(0, 2, 1) for m in attn]
    )
    grad_out_weight = jnp.stack([m[3 * head_width :] for m in attn])
    grad_frames = grad_stream.reshape(clip_count, rows_dev, model_width)
    return (
        output,
        grad_frames,
        grad_qkv,
        grad_bias_pair,
        grad_out_weight,
        grad_up_weight,
        grad_bias_up,
        grad_down_weight,
        own_part(grad_gain_set),
        own_part(grad_shift_set),
    )


def solution(mesh):
    return jax.shard_map(
        on_device,
        mesh=mesh,
        in_specs=(
            P("dp", "seq", None),
            P("dp"),
            P("dp", "seq", None),
            P(None, None, "seq", "head"),
            P(None, None, "head"),
            P(None, "head", "seq"),
            P(None, "seq", "head"),
            P(None, "head"),
            P(None, "head", "seq"),
            P(None, None, "seq"),
            P(None, None, "seq"),
        ),
        out_specs=(
            P("dp", "seq", None),
            P("dp", "seq", None),
            P(None, None, "seq", "head"),
            P(None, None, "head"),
            P(None, "head", "seq"),
            P(None, "seq", "head"),
            P(None, "head"),
            P(None, "head", "seq"),
            P(None, None, "seq"),
            P(None, None, "seq"),
        ),
        check_vma=False,
    )
```
